256 devices in a mesh: seq: 16 (over z_lo, y), tp: 16 (over z_hi, x, core).
Axes of the slice: x: 4, y: 4, z: 8 (z_hi: 2, z_lo: 4; z = z_hi * 4 + z_lo), core: 2. Of those that a mesh axis runs over, the one named last changes fastest.
Arguments:
- hidden: bfloat16 [4096, 4096], P('seq', 'tp'), may hold values from -6 to 6
- attn_gain: float32 [4096], replicated, may hold values from 0.1 to 1.9
- q_weight: bfloat16 [4096, 4096], P(None, 'tp'), may hold values from -0.09375 to 0.09375
- k_weight: bfloat16 [4096, 512], P(None, 'tp'), may hold values from -0.09375 to 0.09375
- v_weight: bfloat16 [4096, 512], P(None, 'tp'), may hold values from -0.09375 to 0.09375
- out_weight: bfloat16 [4096, 4096], P('tp'), may hold values from -0.09375 to 0.09375
- score_gain: float32 [128], replicated, may hold values from 1.5 to 3.5
- stale_keys: bfloat16 [4096, 512], P(None, 'tp'), may hold values from -4 to 4
- stale_values: bfloat16 [4096, 512], P(None, 'tp'), may hold values from -4 to 4
- refresh: int32 [4096], P('seq'), may hold values 0 or 1
- moe_gain: float32 [4096], replicated, may hold values from 0.1 to 1.9
- router: bfloat16 [4096, 16], replicated, may hold values from -0.09375 to 0.09375
- gate_up: bfloat16 [16, 4096, 2048], P('tp', 'seq'), may hold values from -0.09375 to 0.09375
- down: bfloat16 [16, 1024, 4096], P('tp', None, 'seq'), may hold values from -0.1875 to 0.1875
- expert_ids: int32 [4096, 8], P(('seq', 'tp')), may hold values from 0 to 15, all different within a row; in each aligned block of 16 rows (0 to 15, 16 to 31, ...) at most 16 rows name the same one
Outputs:
- mixed: bfloat16 [4096, 4096], P(('seq', 'tp'))
- next_keys: bfloat16 [4096, 512], P(None, 'tp')
- next_values: bfloat16 [4096, 512], P(None, 'tp')
The draws below stay inside these ranges and needn't reach their ends.
Inputs may be any that keep to these rules, and one draw needn't show every extreme that they name: `expert_ids`: among the 16 rows of one device no expert is named more than 16 times, a bound that some block reaches; the 8 experts of a row differ.
All inputs are finite; a program needn't handle non-finite values. No bound on the sum of `refresh` on one device may be relied on, other than what follows from the above.
Results may differ from the reference program's by a relative error of at most 0.015.
Values may be sent and summed in bfloat16 or wider, within the bound.
A program may use at most 128 MiB of HBM per device.

```python
import math
import jax
import jax.numpy as jnp
import numpy as np
from jax import lax

D = 4096
HEADS = 32
KVH = 4
HD = 128
TOPK = 8
FFE = 1024
EXPERTS = 16
TOK_DEV = 256
SEQ = 4096
ROWS = 16
CAP = 16
N_SEQ = 16
N_TP = 16


def set_ends(result, key, smallest, largest):
    place = [jax.random.randint(jax.random.fold_in(key, axis), (), 0, length) for axis, length in enumerate(result.shape)]
    longest = result.shape.index(max(result.shape))
    neighbour = place[:longest] + [(place[longest] + 1) % result.shape[longest]] + place[longest + 1:]
    return result.at[tuple(place)].set(smallest).at[tuple(neighbour)].set(largest)


def block_scale(stream_key, shape, split, least, top_value):
    gain = 1.0
    for position, blocks in split:
        heights = jax.random.uniform(jax.random.fold_in(jax.random.fold_in(stream_key, 6), position), (blocks,), jnp.float32, least / len(split), top_value / len(split))
        gain = gain * jnp.repeat(jnp.exp(heights), shape[position] // blocks).reshape((-1,) + (1,) * (len(shape) - 1 - position))
    return gain


def assign_block(own_key, own, number, rows, number_of, top, bound, lean):
    order = jax.random.permutation(own_key, number_of)
    packed, common = load_shares(number_of, rows * top, bound, lean, True), load_shares(number_of, rows * top, bound, lean, False)
    places = jnp.arange(number_of)

    def named(sizes, offset_by):
        used = int((sizes > 0).sum())
        fixed = max(1, used // 4)
        shifted = fixed + (places - fixed + offset_by * (used - fixed)) % max(1, number_of - fixed)
        return jnp.zeros((number_of,), jnp.int32).at[order[jnp.where(places < fixed, places, shifted)]].set(jnp.asarray(sizes, jnp.int32))

    sizes = jnp.where(number % 4 == 0, named(packed, number // 4), named(common, number - number // 4 - 1))
    mixed = jax.random.permutation(jax.random.fold_in(own, 3), number_of)
    giver, sink = mixed[0:number_of // 2 * 2:2], mixed[1:number_of // 2 * 2:2]
    slack = jnp.minimum(sizes[giver] - 1, bound - sizes[sink]) // 2
    slack = jnp.where((giver == order[0]) | (sink == order[0]) | (sizes[sink] == 0), 0, jnp.maximum(slack, 0))
    shifted = jax.random.randint(jax.random.fold_in(own, 4), (number_of // 2,), 0, 1 << 20) % (slack + 1)
    sizes = sizes.at[giver].add(-shifted).at[sink].add(shifted)
    labels = jnp.searchsorted(jnp.cumsum(sizes), jnp.arange(rows * top), side="right").astype(jnp.int32)
    grid = labels.reshape(top, rows).T
    grid = grid[jax.random.permutation(jax.random.fold_in(own, 1), rows)]
    offset_by = jax.random.randint(jax.random.fold_in(own, 2), (rows, 1), 0, top)
    return jnp.take_along_axis(grid, (jnp.arange(top)[None, :] + offset_by) % top, axis=1)


def load_shares(amount, total, bound, lean, full):
    weights = [(1 << 20) // math.isqrt(rank ** lean) + 1 for rank in range(1, amount + 1)]
    largest = bound if full else min(bound, max(-(-total // amount), total * weights[0] // sum(weights)))
    least = 1 if total - largest >= amount - 1 else 0
    counts, rest = [largest] + [least] * (amount - 1), total - largest - least * (amount - 1)
    while rest > 0:
        free = [i for i in range(1, amount) if counts[i] < largest] or [i for i in range(1, amount) if counts[i] < bound]
        pool, left = sum([weights[i] for i in free]), rest
        for i in free:
            addition = min(bound - counts[i], max(1, left * weights[i] // pool), rest)
            counts[i] = counts[i] + addition
            rest = rest - addition
    return np.array(counts)


def centred(key, extent, spread, most, pieces=(), kind=jnp.bfloat16):
    loudness = block_scale(key, extent, pieces, -0.22, 0.18) if pieces else 1.0
    values = jax.random.normal(key, extent, jnp.float32) * spread * loudness
    return jnp.minimum(jnp.maximum(values, -most), most).astype(kind)


def setup_inputs(seed: int = 0) -> dict:
    key_of = jax.random.split(jax.random.key(seed), 16)
    hidden = centred(key_of[0], (SEQ, D), 1.0, 6.0, ((0, 16), (1, 16)))
    attn_gain = jnp.clip(1.0 + 0.18 * jax.random.normal(key_of[1], (D,), jnp.float32), 0.1, 1.9)
    q_weight = centred(key_of[2], (D, HEADS * HD), D ** -0.5, 0.09375, ((1, 16),))
    k_weight = centred(key_of[3], (D, KVH * HD), D ** -0.5, 0.09375, ((1, 16),))
    v_weight = centred(key_of[4], (D, KVH * HD), D ** -0.5, 0.09375, ((1, 16),))
    out_weight = centred(key_of[5], (HEADS * HD, D), (HEADS * HD) ** -0.5, 0.09375, ((0, 16),))
    score_gain = jnp.clip(jnp.exp(jax.random.uniform(key_of[6], (HD,), jnp.float32, math.log(1.5), math.log(3.5))), 1.5, 3.5)
    stale_keys = centred(key_of[7], (SEQ, KVH * HD), 1.0, 4.0, ((1, 16),))
    stale_values = centred(key_of[8], (SEQ, KVH * HD), 1.0, 4.0, ((1, 16),))
    refresh = set_ends((jax.random.randint(key_of[9], (SEQ,), 0, 2) < 1).astype(jnp.int32), jax.random.fold_in(key_of[9], 1), 0, 1)
    moe_gain = jnp.clip(1.0 + 0.18 * jax.random.normal(key_of[10], (D,), jnp.float32), 0.1, 1.9)
    router = centred(key_of[11], (D, EXPERTS), D ** -0.5, 0.09375)
    gate_up = centred(key_of[12], (EXPERTS, D, 2 * FFE), D ** -0.5, 0.09375, ((0, 16), (1, 16)))
    down = centred(key_of[13], (EXPERTS, FFE, D), FFE ** -0.5, 0.1875, ((0, 16), (2, 16)))
    expert_ids_keys = jax.random.split(jax.random.fold_in(key_of[14], 1), SEQ // ROWS)
    expert_ids_turns = jax.random.permutation(jax.random.fold_in(key_of[14], 3), SEQ // ROWS)
    expert_ids = jax.vmap(lambda own, number: assign_block(jax.random.fold_in(key_of[14], 2), own, number, ROWS, EXPERTS, TOPK, CAP, 2))(expert_ids_keys, expert_ids_turns).reshape((SEQ, TOPK))
    return {"hidden": hidden, "attn_gain": attn_gain, "q_weight": q_weight, "k_weight": k_weight, "v_weight": v_weight, "out_weight": out_weight, "score_gain": score_gain, "stale_keys": stale_keys, "stale_values": stale_values, "refresh": refresh, "moe_gain": moe_gain, "router": router, "gate_up": gate_up, "down": down, "expert_ids": expert_ids}


def normalize(values):
    return values * lax.rsqrt(lax.optimization_barrier(jnp.mean(values * values, axis=-1, keepdims=True)) + 1e-06)

def reference(hidden, attn_gain, q_weight, k_weight, v_weight, out_weight, score_gain, stale_keys, stale_values, refresh, moe_gain, router, gate_up, down, expert_ids):
    inputs = hidden.astype(jnp.float32)
    normed = (normalize(inputs) * attn_gain).astype(jnp.bfloat16)
    queries = jnp.dot(normed, q_weight, preferred_element_type=jnp.float32).reshape(SEQ, HEADS, HD)
    queries = (normalize(queries) * score_gain * (1.0 / math.sqrt(HD))).astype(jnp.bfloat16)
    fresh_keys = jnp.dot(normed, k_weight, preferred_element_type=jnp.float32).astype(jnp.bfloat16)
    fresh_values = jnp.dot(normed, v_weight, preferred_element_type=jnp.float32).astype(jnp.bfloat16)
    refreshed = (refresh == 1)[:, None]
    next_keys = jnp.where(refreshed, fresh_keys, stale_keys)
    next_values = jnp.where(refreshed, fresh_values, stale_values)
    per_group = HEADS // KVH

    def one_head(head):
        column = head // per_group * HD
        old_keys = lax.dynamic_slice_in_dim(stale_keys, column, HD, 1)
        old_values = lax.dynamic_slice_in_dim(stale_values, column, HD, 1)
        new_keys = lax.dynamic_slice_in_dim(fresh_keys, column, HD, 1)
        new_values = lax.dynamic_slice_in_dim(fresh_values, column, HD, 1)
        query_head = lax.dynamic_index_in_dim(queries, head, 1, keepdims=False)

        def one_block(block):
            start = (block * TOK_DEV).astype(jnp.int32)
            keys = lax.dynamic_update_slice_in_dim(old_keys, lax.dynamic_slice_in_dim(new_keys, start, TOK_DEV, 0), start, 0)
            values = lax.dynamic_update_slice_in_dim(old_values, lax.dynamic_slice_in_dim(new_values, start, TOK_DEV, 0), start, 0)
            keys = normalize(keys.astype(jnp.float32)).astype(jnp.bfloat16)
            block_queries = lax.dynamic_slice_in_dim(query_head, start, TOK_DEV, 0)
            scores = jnp.einsum('td,sd->ts', block_queries.astype(jnp.float32), keys.astype(jnp.float32))
            weights = jnp.exp(scores)
            total = lax.optimization_barrier(jnp.sum(weights, axis=1))
            probs = lax.optimization_barrier(weights.astype(jnp.bfloat16))
            numer = jnp.einsum('ts,sd->td', probs.astype(jnp.float32), values.astype(jnp.float32))
            return (numer / total[:, None]).astype(jnp.bfloat16)
        return lax.map(one_block, jnp.arange(N_SEQ, dtype=jnp.int32)).reshape(SEQ, HD)
    heads_out = lax.map(one_head, jnp.arange(HEADS, dtype=jnp.int32))
    heads_out = jnp.transpose(heads_out, (1, 0, 2)).reshape(SEQ, HEADS * HD)
    width = HEADS * HD // N_TP

    def add_group(total, group):
        start = (group * width).astype(jnp.int32)
        columns = lax.dynamic_slice_in_dim(heads_out, start, width, 1)
        weight_rows = lax.dynamic_slice_in_dim(out_weight, start, width, 0)
        term = lax.optimization_barrier(jnp.dot(columns, weight_rows, preferred_element_type=jnp.float32).astype(jnp.bfloat16))
        return (total + term.astype(jnp.float32), None)
    attended, _ = lax.scan(add_group, jnp.zeros((SEQ, D), jnp.float32), jnp.arange(N_TP, dtype=jnp.int32))
    residual = inputs + attended
    moe_in = (normalize(residual) * moe_gain).astype(jnp.bfloat16)
    logits = jnp.dot(moe_in, router, preferred_element_type=jnp.float32)
    chosen = jax.nn.sigmoid(jnp.take_along_axis(logits, expert_ids, axis=1))
    gates = 2.5 * chosen / lax.optimization_barrier(jnp.sum(chosen, axis=1, keepdims=True))

    def add_expert(total, expert):
        token_weight = lax.optimization_barrier(jnp.sum(jnp.where(expert_ids == expert, gates, 0.0), axis=1))
        projected = jnp.dot(moe_in, gate_up[expert], preferred_element_type=jnp.float32)
        acted = (jax.nn.silu(projected[:, :FFE]) * projected[:, FFE:]).astype(jnp.bfloat16)
        expert_out = lax.optimization_barrier(jnp.dot(acted, down[expert], preferred_element_type=jnp.float32).astype(jnp.bfloat16))
        return (total + token_weight[:, None] * expert_out.astype(jnp.float32), None)
    moe_sum, _ = lax.scan(add_expert, jnp.zeros((SEQ, D), jnp.float32), jnp.arange(EXPERTS, dtype=jnp.int32))
    mixed = (residual + moe_sum).astype(jnp.bfloat16)
    return (mixed, next_keys, next_values)
```

```python
import functools
import math

import jax
import jax.numpy as jnp
from jax import lax
from jax.experimental import pallas as pl
from jax.experimental.pallas import tpu as pltpu
from jax.sharding import PartitionSpec as P

HD = 128
MESH = pl.DeviceIdType.MESH
F32 = jnp.float32
BF16 = jnp.bfloat16
NT = (((1,), (1,)), ((), ()))
EPS = 1e-06
NCH = 4
COPIES = 160


class Copies:
    def __init__(self, send, recv):
        self.send, self.recv, self.all = send, recv, []

    def __call__(self, src, dst, device):
        k = len(self.all)
        copy = pltpu.make_async_remote_copy(
            src_ref=src,
            dst_ref=dst,
            send_sem=self.send.at[k],
            recv_sem=self.recv.at[k],
            device_id=device,
            device_id_type=MESH,
        )
        copy.start()
        self.all.append(copy)
        return copy


def kernel(
    hidden,
    attn_gain,
    q_weight,
    kw_t,
    vw_t,
    out_weight,
    score_gain,
    sk_t,
    sv_t,
    refresh,
    moe_gain,
    router_t,
    gate_up,
    down,
    ids_t,
    mixed,
    next_k,
    next_v,
    hid,
    qw,
    ow,
    kt,
    vt,
    queries,
    total,
    numer,
    fresh,
    nkv,
    heads,
    resid,
    moe_in,
    ag,
    pay,
    gu,
    dn,
    psend,
    precv,
    pown,
    act,
    gate_w,
    sib_s1,
    sib_r1,
    own1,
    xs1,
    xr1,
    zs1,
    zr1,
    zo1,
    sib_s2,
    sib_r2,
    own2,
    xs2,
    xr2,
    zs2,
    zr2,
    zo2,
    fsend,
    frecv,
    send_sems,
    recv_sems,
    local_sems,
):
    s = lax.axis_index("seq")
    t = lax.axis_index("tp")
    y, zl = s % 4, s // 4
    zh, x, c = t // 8, (t // 2) % 4, t % 2
    half = zl % 2
    j = t % 4
    sibling = (s, t - c + (1 - c))
    zpartner = (s, (t + 8) % 16)
    xpair = x + 1 - 2 * (x % 2)
    xmate = (s, zh * 8 + xpair * 2 + c)
    xmate_sib = (s, zh * 8 + xpair * 2 + (1 - c))
    zpair = (s + 4 - 8 * half, t)
    zfar = ((s + 8) % 16, t)

    def xdev(d):
        return (s, zh * 8 + ((x + d) % 4) * 2 + c)

    def ydev(d):
        return (zl * 4 + (y + d) % 4, t)

    def seqdev(d):
        return ((s + d) % 16, t)

    partners = [sibling, zpartner, xmate_sib] + [xdev(d) for d in (1, 2, 3)]
    partners += [seqdev(d) for d in range(1, 16)]
    barrier = pltpu.get_barrier_semaphore()
    for device in partners:
        pl.semaphore_signal(barrier, inc=1, device_id=device, device_id_type=MESH)

    locals_ = []

    def local(src, dst):
        copy = pltpu.make_async_copy(src, dst, local_sems.at[len(locals_)])
        copy.start()
        locals_.append(copy)
        return copy

    l_hid = local(hidden, hid.at[t])
    l_k = local(sk_t, kt.at[pl.ds(pl.multiple_of(j * 32, 32), 32)])
    l_v = local(sv_t, vt.at[pl.ds(pl.multiple_of(j * 32, 32), 32)])
    l_q = local(q_weight, qw)
    l_o = local(out_weight, ow)
    own_gu = gu.at[(zl // 2) * 4 + y]
    own_dn = dn.at[(zl // 2) * 4 + y]
    l_gu = local(gate_up, own_gu)
    l_dn = local(down, own_dn)

    pl.semaphore_wait(barrier, len(partners))
    copies = Copies(send_sems, recv_sems)

    def gather_start(buf, src, slot):
        own = slot(zh, x, c)
        a = copies(src, buf.at[own], zpartner)
        b = {d: copies(src, buf.at[own], xdev(d)) for d in (1, 3, 2)}
        return a, b, [copies(src, buf.at[own], sibling)]

    def gather_finish(buf, slot, started, between=lambda: None):
        a, b, to_sib = started
        a.wait_recv()
        far = buf.at[slot(1 - zh, x, c)]
        e = {d: copies(far, far, xdev(d)) for d in (1, 3, 2)}
        to_sib.append(copies(far, far, sibling))
        between()
        for z_of, group in ((zh, b), (1 - zh, e)):
            for d in (1, 3, 2):
                group[d].wait_recv()
                part = buf.at[slot(z_of, (x + 4 - d) % 4, c)]
                to_sib.append(copies(part, part, sibling))
        for copy in to_sib:
            copy.wait_recv()

    by_index = lambda zh_, x_, c_: zh_ * 8 + x_ * 2 + c_
    started = gather_start(hid, hidden, by_index)
    krows = kt.at[pl.ds(pl.multiple_of(j * 32, 32), 32)]
    vrows = vt.at[pl.ds(pl.multiple_of(j * 32, 32), 32)]
    kx = copies(sk_t, krows, xmate)
    vx = copies(sv_t, vrows, xmate)
    stale = [copies(sk_t, krows, sibling), copies(sv_t, vrows, sibling)]
    gu_y = [copies(gate_up, own_gu, ydev(d)) for d in (1, 3, 2)]
    gu_z = []

    def after_z():
        gu_z.append(copies(gate_up, own_gu, zfar))

    gather_finish(hid, by_index, started, after_z)
    jx = (xpair % 2) * 2 + c
    kx.wait_recv()
    kxr = kt.at[pl.ds(pl.multiple_of(jx * 32, 32), 32)]
    stale.append(copies(kxr, kxr, sibling))
    vx.wait_recv()
    vxr = vt.at[pl.ds(pl.multiple_of(jx * 32, 32), 32)]
    stale.append(copies(vxr, vxr, sibling))

    l_hid.wait()
    l_q.wait()
    sq = jnp.zeros((256, 128), F32)
    for k in range(16):
        v = hid[k].astype(F32)
        v = v * v
        sq = sq + v[:, :128] + v[:, 128:]
    inv = lax.rsqrt(jnp.sum(sq, axis=1, keepdims=True) / 4096.0 + EPS)
    q = jnp.zeros((256, 256), F32)
    kv = jnp.zeros((64, 256), F32)
    for k in range(16):
        cols = slice(k * 256, (k + 1) * 256)
        n = (hid[k].astype(F32) * inv * attn_gain[:, cols]).astype(BF16)
        q = q + jnp.dot(n, qw[cols, :], preferred_element_type=F32)
        w = jnp.concatenate([kw_t[:, cols], vw_t[:, cols]], axis=0)
        kv = kv + lax.dot_general(w, n, NT, preferred_element_type=F32)
    kv = kv.astype(BF16)
    fresh[j] = kv
    for_mates = [copies(fresh.at[j], fresh.at[j], d) for d in (sibling, xmate, xmate_sib)]
    for h in range(2):
        qh = q[:, h * HD : (h + 1) * HD]
        r = lax.rsqrt(jnp.mean(qh * qh, axis=1, keepdims=True) + EPS)
        queries[h * 256 : (h + 1) * 256, :] = (
            qh * r * score_gain[...] * (1.0 / math.sqrt(HD))
        ).astype(BF16)
    rows = pl.ds(pl.multiple_of(t * 16, 16), 16)
    for k in range(16):
        resid[:, k * 256 : (k + 1) * 256] = hid[k, rows, :].astype(F32)

    l_k.wait()
    l_v.wait()
    block = pl.ds(pl.multiple_of(s * 256, 256), 256)
    old = jnp.concatenate([sk_own(kt, j, block), sk_own(vt, j, block)], axis=0)
    nkv[s] = jnp.where(refresh[...] == 1, kv.astype(F32), old.astype(F32)).astype(BF16)

    for copy in stale:
        copy.wait_recv()
    total[...] = jnp.zeros_like(total)
    numer[...] = jnp.zeros_like(numer)

    def attend(kb, vb):
        kb = kb.astype(F32)
        r = lax.rsqrt(jnp.mean(kb * kb, axis=0, keepdims=True) + EPS)
        kn = (kb * r).astype(BF16)
        w = jnp.exp(jnp.dot(queries[...], kn, preferred_element_type=F32))
        total[...] += w[:, :128] + w[:, 128:]
        numer[...] += lax.dot_general(w.astype(BF16), vb, NT, preferred_element_type=F32)

    def other_block(i, carry):
        b = (s + 1 + i) % 16
        cols = pl.ds(pl.multiple_of(b * 256, 256), 256)
        attend(kt[:, cols], vt[:, cols])
        return carry

    lax.fori_loop(0, 15, other_block, 0)
    for copy in for_mates:
        copy.wait_recv()
    fr = fresh[...]
    attend(fr[:, :32].reshape(128, 256), fr[:, 32:].reshape(128, 256))
    for h in range(2):
        hr = slice(h * 256, (h + 1) * 256)
        den = jnp.sum(total[hr, :], axis=1, keepdims=True)
        o = (numer[hr, :] / den).astype(BF16).reshape(8, 2, 16, HD)
        for cc in range(2):
            heads[cc, :, h * HD : (h + 1) * HD] = o[:, cc].reshape(128, HD)

    for copy in gu_z:
        copy.wait_recv()
    far_gu = gu.at[(1 - zl // 2) * 4 + y]
    gu_y += [copies(far_gu, far_gu, ydev(d)) for d in (1, 3, 2)]

    def reduce_scatter(nb, width, produce, sib_s, sib_r, own, xs, xr, zs, zr, zo, finish):
        to_sib, to_x, to_z = [], [], []
        for k in range(NCH):
            sib_s[k] = produce(1 - c, k).astype(BF16)
            to_sib.append(copies(sib_s.at[k], sib_r.at[k], sibling))
        for k in range(NCH):
            v = produce(c, k)
            to_sib[k].wait_recv()
            v = (v + sib_r[k].astype(F32)).reshape(nb * 2, 4, 16, width)
            own[k] = v
            xs[k] = v.astype(BF16)
            to_x.append(
                [
                    copies(xs.at[k, :, (x + d) % 4], xr.at[k, d - 1], xdev(d))
                    for d in (1, 3, 2)
                ]
            )
        for k in range(NCH):
            v = own[k, :, x]
            for copy in to_x[k]:
                copy.wait_recv()
            for d in range(3):
                v = v + xr[k, d].astype(F32)
            v = v.reshape(nb, 2, 16, width)
            lo, hi = v[:, 0], v[:, 1]
            zs[k] = jnp.where(zh == 0, hi, lo).astype(BF16)
            zo[k] = jnp.where(zh == 0, lo, hi)
            to_z.append(copies(zs.at[k], zr.at[k], zpartner))
        for k in range(NCH):
            to_z[k].wait_recv()
            finish(k, zo[k] + zr[k].astype(F32))

    l_o.wait()

    def project(cc, k):
        return jnp.dot(
            heads[cc], ow[:, k * 1024 : (k + 1) * 1024], preferred_element_type=F32
        )

    def add_attended(k, v):
        resid[:, k * 1024 : (k + 1) * 1024] += v[0]

    reduce_scatter(
        1, 1024, project, sib_s1, sib_r1, own1, xs1, xr1, zs1, zr1, zo1, add_attended
    )
    dn_y = [copies(down, own_dn, ydev(d)) for d in (1, 3, 2)]

    v = resid[...]
    inv = lax.rsqrt(jnp.mean(v * v, axis=1, keepdims=True) + EPS)
    m = (v * inv * moe_gain[...]).astype(BF16)
    logits = lax.dot_general(router_t[...], m, NT, preferred_element_type=F32)
    expert = lax.broadcasted_iota(jnp.int32, (16, 16), 0)
    picked = jnp.zeros((16, 16), F32)
    for k in range(8):
        picked = picked + jnp.where(expert == ids_t[k : k + 1, :], 1.0, 0.0)
    sig = picked / (1.0 + jnp.exp(-logits))
    gates = 2.5 * sig / jnp.sum(sig, axis=0, keepdims=True)
    high = gates.astype(BF16).astype(F32)
    both = jnp.concatenate([high, gates - high, jnp.zeros((96, 16), F32)], axis=0)
    gates_rows = jnp.transpose(both).astype(BF16)
    for k in range(4):
        moe_in[k] = m[:, k * 1024 : (k + 1) * 1024]
    sigma = lambda zh_, x_, c_: c_ * 8 + zh_ * 4 + x_
    mine = sigma(zh, x, c)
    pay[:, :1024] = moe_in[1 - half]
    pay[:, 1024:2048] = moe_in[3 - half]
    pay[:, 2048:] = gates_rows
    swap = copies(pay, ag.at[mine, 1], zpair)
    dn_z = copies(down, own_dn, zfar)
    ag[mine, 0, :, :1024] = moe_in[half]
    ag[mine, 0, :, 1024:2048] = moe_in[half + 2]
    ag[mine, 0, :, 2048:] = gates_rows
    swap.wait_recv()
    started = gather_start(ag, ag.at[mine], sigma)
    gather_finish(ag, sigma, started)

    to_seq = [copies(nkv.at[s], nkv.at[s], seqdev(d)) for d in range(1, 16)]

    l_gu.wait()
    for copy in gu_y:
        copy.wait_recv()
    dn_z.wait_recv()
    far_dn = dn.at[(1 - zl // 2) * 4 + y]
    dn_y += [copies(far_dn, far_dn, ydev(d)) for d in (1, 3, 2)]
    lane = lax.broadcasted_iota(jnp.int32, (256, 128), 1)
    is_mine = (lane == t) | (lane == t + 16)

    def partial(b, k, i):
        a = ag[:, b, :, :2048].reshape(256, 2048)
        cols = slice(i * 1024 + k * 256, i * 1024 + (k + 1) * 256)
        return jnp.dot(a, gu[:, :, cols].reshape(2048, 256), preferred_element_type=F32)

    to_pair = []
    for k in range(4):
        for i in range(2):
            psend[k, i] = partial(1, k, i).astype(BF16)
        to_pair.append(copies(psend.at[k], precv.at[k], zpair))
    for k in range(4):
        for i in range(2):
            pown[k, i] = partial(0, k, i)
    for b in range(2):
        w = ag[:, b, :, 2048:].reshape(256, 128).astype(F32)
        gate_w[b] = jnp.sum(jnp.where(is_mine, w, 0.0), axis=1, keepdims=True)
    back = []
    for k in range(4):
        to_pair[k].wait_recv()
        g = pown[k, 0] + precv[k, 0].astype(F32)
        u = pown[k, 1] + precv[k, 1].astype(F32)
        act[0, k] = (g / (1.0 + jnp.exp(-g)) * u).astype(BF16)
        back.append(copies(act.at[0, k], act.at[1, k], zpair))
    for copy in back:
        copy.wait_recv()

    l_dn.wait()
    for copy in dn_y:
        copy.wait_recv()

    def expert_out(cc, k):
        r = pl.ds(pl.multiple_of(cc * 128, 128), 128)
        a = [act[:, i, r, :].reshape(256, 256) for i in range(4)]
        w = gate_w[:, r, :].reshape(256, 1)
        outs = []
        for n in (2 * k, 2 * k + 1):
            o = jnp.zeros((256, 256), F32)
            for i in range(4):
                o = o + jnp.dot(
                    a[i], dn[n, i * 256 : (i + 1) * 256, :], preferred_element_type=F32
                )
            outs.append(o * w)
        return jnp.concatenate(outs, axis=1)

    final = []

    def to_owner(k, v):
        fsend[k] = v[1].astype(BF16)
        final.append((copies(fsend.at[k], frecv.at[k], zpair), v[0]))

    reduce_scatter(
        2, 512, expert_out, sib_s2, sib_r2, own2, xs2, xr2, zs2, zr2, zo2, to_owner
    )
    for k in range(4):
        copy, v = final[k]
        near = (k // 2) * 2048 + (k % 2) * 512
        cols = pl.ds(pl.multiple_of(near + half * 1024, 512), 512)
        mixed[:, cols] = (resid[:, cols] + v).astype(BF16)
        copy.wait_recv()
        cols = pl.ds(pl.multiple_of(near + (1 - half) * 1024, 512), 512)
        mixed[:, cols] = (resid[:, cols] + frecv[k].astype(F32)).astype(BF16)

    for copy in to_seq:
        copy.wait_recv()
    for k in range(16):
        next_k[:, k * 256 : (k + 1) * 256] = nkv[k, :32]
        next_v[:, k * 256 : (k + 1) * 256] = nkv[k, 32:]
    for copy in copies.all:
        copy.wait_send()


def sk_own(ref, j, block):
    return ref[pl.ds(pl.multiple_of(j * 32, 32), 32), block]


def on_device(
    hidden,
    attn_gain,
    q_weight,
    k_weight,
    v_weight,
    out_weight,
    score_gain,
    stale_keys,
    stale_values,
    refresh,
    moe_gain,
    router,
    gate_up,
    down,
    expert_ids,
):
    anywhere = pl.BlockSpec(memory_space=pl.ANY)
    vmem = pl.BlockSpec(memory_space=pltpu.VMEM)

    def rs(nb, width):
        return [
            pltpu.VMEM((NCH, nb * 128, width), BF16),
            pltpu.VMEM((NCH, nb * 128, width), BF16),
            pltpu.VMEM((NCH, nb * 2, 4, 16, width), F32),
            pltpu.VMEM((NCH, nb * 2, 4, 16, width), BF16),
            pltpu.VMEM((NCH, 3, nb * 2, 16, width), BF16),
            pltpu.VMEM((NCH, nb, 16, width), BF16),
            pltpu.VMEM((NCH, nb, 16, width), BF16),
            pltpu.VMEM((NCH, nb, 16, width), F32),
        ]

    mixed, next_k, next_v = pl.pallas_call(
        kernel,
        out_shape=(
            jax.ShapeDtypeStruct((16, 4096), BF16),
            jax.ShapeDtypeStruct((32, 4096), BF16),
            jax.ShapeDtypeStruct((32, 4096), BF16),
        ),
        in_specs=[
            anywhere,
            vmem,
            anywhere,
            vmem,
            vmem,
            anywhere,
            vmem,
            anywhere,
            anywhere,
            vmem,
            vmem,
            vmem,
            anywhere,
            anywhere,
            vmem,
        ],
        out_specs=(vmem, vmem, vmem),
        scratch_shapes=[
            pltpu.VMEM((16, 256, 256), BF16),
            pltpu.VMEM((4096, 256), BF16),
            pltpu.VMEM((256, 4096), BF16),
            pltpu.VMEM((128, 4096), BF16),
            pltpu.VMEM((128, 4096), BF16),
            pltpu.VMEM((512, 128), BF16),
            pltpu.VMEM((512, 128), F32),
            pltpu.VMEM((512, 128), F32),
            pltpu.VMEM((4, 64, 256), BF16),
            pltpu.VMEM((16, 64, 256), BF16),
            pltpu.VMEM((2, 128, 256), BF16),
            pltpu.VMEM((16, 4096), F32),
            pltpu.VMEM((4, 16, 1024), BF16),
            pltpu.VMEM((16, 2, 16, 2176), BF16),
            pltpu.VMEM((16, 2176), BF16),
            pltpu.VMEM((8, 256, 2048), BF16),
            pltpu.VMEM((8, 1024, 256), BF16),
            pltpu.VMEM((4, 2, 256, 256), BF16),
            pltpu.VMEM((4, 2, 256, 256), BF16),
            pltpu.VMEM((4, 2, 256, 256), F32),
            pltpu.VMEM((2, 4, 256, 256), BF16),
            pltpu.VMEM((2, 256, 1), F32),
            *rs(1, 1024),
            *rs(2, 512),
            pltpu.VMEM((NCH, 16, 512), BF16),
            pltpu.VMEM((NCH, 16, 512), BF16),
            pltpu.SemaphoreType.DMA((COPIES,)),
            pltpu.SemaphoreType.DMA((COPIES,)),
            pltpu.SemaphoreType.DMA((8,)),
        ],
        compiler_params=pltpu.CompilerParams(
            collective_id=0, has_side_effects=True, vmem_limit_bytes=60 * 2**20
        ),
    )(
        hidden,
        attn_gain.reshape(1, -1),
        q_weight,
        k_weight.T,
        v_weight.T,
        out_weight,
        score_gain.reshape(1, -1),
        stale_keys.T,
        stale_values.T,
        refresh.reshape(1, -1),
        moe_gain.reshape(1, -1),
        router.T,
        gate_up[0],
        down[0],
        expert_ids.T,
    )
    return (mixed, next_k.T, next_v.T)


def solution(mesh):
    placed = (
        P("seq", "tp"),
        P(),
        P(None, "tp"),
        P(None, "tp"),
        P(None, "tp"),
        P("tp", None),
        P(),
        P(None, "tp"),
        P(None, "tp"),
        P("seq"),
        P(),
        P(),
        P("tp", "seq", None),
        P("tp", None, "seq"),
        P(("seq", "tp"), None),
    )
    return jax.shard_map(
        on_device,
        mesh=mesh,
        in_specs=placed,
        out_specs=(P(("seq", "tp"), None), P(None, "tp"), P(None, "tp")),
        check_vma=False,
    )
```

```python
import functools
import math

import jax
import jax.numpy as jnp
from jax import lax
from jax.experimental import pallas as pl
from jax.experimental.pallas import tpu as pltpu
from jax.sharding import PartitionSpec as P

HD = 128
MESH = pl.DeviceIdType.MESH
F32 = jnp.float32
BF16 = jnp.bfloat16
NT = (((1,), (1,)), ((), ()))
EPS = 1e-06
NCH = 4
COPIES = 160
SCHEDULE = {
    "start": [("gu", "near", 0, 256), ("gu", "z", 0, 128)],
    "far hidden": [("gu", "z", 128, 128)],
    "hidden": [("gu", "near on", 0, 256)],
    "attended": [("dn", "near", 0, 1024)],
    "sum along x": [("gu", "far", 0, 128)],
    "sum along z": [("gu", "far", 128, 128), ("gu", "far on", 0, 128)],
    "far rows": [("dn", "z", 0, 1024), ("gu", "far on", 128, 128)],
    "rows": [("dn", "near on", 0, 1024)],
    "acted 0": [("dn", "far", 0, 1024)],
    "acted 3": [("dn", "far on", 0, 1024)],
}


class Copies:
    def __init__(self, send, recv):
        self.send, self.recv, self.all = send, recv, []

    def __call__(self, src, dst, device):
        k = len(self.all)
        copy = pltpu.make_async_remote_copy(
            src_ref=src,
            dst_ref=dst,
            send_sem=self.send.at[k],
            recv_sem=self.recv.at[k],
            device_id=device,
            device_id_type=MESH,
        )
        copy.start()
        self.all.append(copy)
        return copy


def kernel(
    hidden,
    attn_gain,
    q_weight,
    kw_t,
    vw_t,
    out_weight,
    score_gain,
    sk_t,
    sv_t,
    refresh,
    moe_gain,
    router_t,
    gate_up,
    down,
    ids_t,
    mixed,
    next_k,
    next_v,
    hid,
    qw,
    ow,
    kt,
    vt,
    queries,
    total,
    numer,
    fresh,
    nkv,
    heads,
    resid,
    moe_in,
    ag0,
    ag1,
    pay,
    gu,
    dn,
    psend,
    precv,
    pown,
    act,
    sib_s1,
    sib_r1,
    own1,
    xs1,
    xr1,
    zs1,
    zr1,
    zo1,
    sib_s2,
    sib_r2,
    own2,
    xs2,
    xr2,
    zs2,
    zr2,
    zo2,
    fsend,
    frecv,
    send_sems,
    recv_sems,
    local_sems,
):
    s = lax.axis_index("seq")
    t = lax.axis_index("tp")
    y, zl = s % 4, s // 4
    zh, x, c = t // 8, (t // 2) % 4, t % 2
    half = zl % 2
    j = t % 4
    sibling = (s, t - c + (1 - c))
    zpartner = (s, (t + 8) % 16)
    xpair = x + 1 - 2 * (x % 2)
    xmate = (s, zh * 8 + xpair * 2 + c)
    xmate_sib = (s, zh * 8 + xpair * 2 + (1 - c))
    zpair = (s + 4 - 8 * half, t)
    zfar = ((s + 8) % 16, t)

    def xdev(d):
        return (s, zh * 8 + ((x + d) % 4) * 2 + c)

    def ydev(d):
        return (zl * 4 + (y + d) % 4, t)

    partners = [sibling, zpartner, xmate_sib, zpair, zfar]
    partners += [xdev(d) for d in (1, 2, 3)] + [ydev(d) for d in (1, 2, 3)]
    barrier = pltpu.get_barrier_semaphore()
    for device in partners:
        pl.semaphore_signal(barrier, inc=1, device_id=device, device_id_type=MESH)

    locals_ = []

    def local(src, dst):
        copy = pltpu.make_async_copy(src, dst, local_sems.at[len(locals_)])
        copy.start()
        locals_.append(copy)
        return copy

    l_hid = local(hidden, hid.at[t])
    l_k = local(sk_t, kt.at[pl.ds(pl.multiple_of(j * 32, 32), 32)])
    l_v = local(sv_t, vt.at[pl.ds(pl.multiple_of(j * 32, 32), 32)])
    l_q = local(q_weight, qw)
    l_o = local(out_weight, ow)
    own_gu = gu.at[(zl // 2) * 4 + y]
    own_dn = dn.at[half * 4 + y]
    l_gu = local(gate_up, own_gu)
    l_dn = local(down, own_dn)

    pl.semaphore_wait(barrier, len(partners))
    copies = Copies(send_sems, recv_sems)

    def gather_start(view, src):
        own = view(zh, x, c)
        over_z = copies(src, own, zpartner)
        over_x = {d: copies(src, own, xdev(d)) for d in (1, 3, 2)}
        return view, over_z, [(zh, over_x)], [copies(src, own, sibling)]

    def gather_z(gather):
        view, over_z, over_x, to_sib = gather
        over_z.wait_recv()
        far = view(1 - zh, x, c)
        over_x.append((1 - zh, {d: copies(far, far, xdev(d)) for d in (1, 3, 2)}))
        to_sib.append(copies(far, far, sibling))

    def gather_x(gather, k):
        view, _, over_x, to_sib = gather
        z_of, group = over_x[k]
        for d in (1, 3, 2):
            group[d].wait_recv()
            part = view(z_of, (x + 4 - d) % 4, c)
            to_sib.append(copies(part, part, sibling))

    def gather_end(gather):
        for copy in gather[3]:
            copy.wait_recv()

    def ring_start(buf, src, zz, first, rows_):
        run = pl.ds(first, rows_)
        dst = buf.at[zz * 4 + y, run]
        return [copies(src.at[run], dst, ydev(d)) for d in (1, 3)]

    def ring_relay(buf, zz, first, rows_, started):
        sent = []
        for copy, d, start in zip(started, (1, 3), (first, first + rows_ // 2)):
            copy.wait_recv()
            part = buf.at[zz * 4 + (y + 4 - d) % 4, pl.ds(start, rows_ // 2)]
            sent.append(copies(part, part, ydev(d)))
        return sent

    bulk, ready = {}, {"gu": [], "dn": []}

    def at(point):
        for name, step, first, rows_ in SCHEDULE.get(point, ()):
            if name == "gu":
                buf, src, near, over = gu, gate_up, zl // 2, zfar
            else:
                buf, src, near, over = dn, down, half, zpair
            run = pl.ds(first, rows_)
            if step == "near":
                bulk[name, first] = ring_start(buf, src, near, first, rows_)
            elif step == "near on":
                ready[name] += ring_relay(buf, near, first, rows_, bulk[name, first])
            elif step == "z":
                own = buf.at[near * 4 + y, run]
                bulk[name, "z", first] = copies(src.at[run], own, over)
            elif step == "far":
                bulk[name, "z", first].wait_recv()
                far = buf.at[(1 - near) * 4 + y]
                bulk[name, "f", first] = ring_start(buf, far, 1 - near, first, rows_)
            else:
                ready[name] += ring_relay(
                    buf, 1 - near, first, rows_, bulk[name, "f", first]
                )

    gathers = []
    for first in (0, 128):
        rows_ = pl.ds(first, 128)
        gathers.append(
            gather_start(
                lambda zh_, x_, c_, rows_=rows_: hid.at[zh_ * 8 + x_ * 2 + c_, rows_],
                hidden.at[rows_],
            )
        )
    krows = kt.at[pl.ds(pl.multiple_of(j * 32, 32), 32)]
    vrows = vt.at[pl.ds(pl.multiple_of(j * 32, 32), 32)]
    kx = copies(sk_t, krows, xmate)
    stale = [copies(sk_t, krows, sibling), copies(sv_t, vrows, sibling)]
    at("start")
    for g in gathers:
        gather_z(g)
    vx = copies(sv_t, vrows, xmate)
    at("far hidden")
    for k in range(2):
        for g in gathers:
            gather_x(g, k)
    jx = (xpair % 2) * 2 + c
    kx.wait_recv()
    kxr = kt.at[pl.ds(pl.multiple_of(jx * 32, 32), 32)]
    stale.append(copies(kxr, kxr, sibling))
    for g in gathers:
        gather_end(g)
    l_hid.wait()
    at("hidden")

    l_q.wait()
    sq = jnp.zeros((256, 128), F32)
    for k in range(16):
        v = hid[k].astype(F32)
        v = v * v
        sq = sq + v[:, :128] + v[:, 128:]
    inv = lax.rsqrt(jnp.sum(sq, axis=1, keepdims=True) / 4096.0 + EPS)
    q = jnp.zeros((256, 256), F32)
    kv = jnp.zeros((64, 256), F32)
    for k in range(16):
        cols = slice(k * 256, (k + 1) * 256)
        n = (hid[k].astype(F32) * inv * attn_gain[:, cols]).astype(BF16)
        q = q + jnp.dot(n, qw[cols, :], preferred_element_type=F32)
        w = jnp.concatenate([kw_t[:, cols], vw_t[:, cols]], axis=0)
        kv = kv + lax.dot_general(w, n, NT, preferred_element_type=F32)
    kv = kv.astype(BF16)
    fresh[j] = kv
    for_mates = [copies(fresh.at[j], fresh.at[j], d) for d in (sibling, xmate, xmate_sib)]
    for h in range(2):
        qh = q[:, h * HD : (h + 1) * HD]
        r = lax.rsqrt(jnp.mean(qh * qh, axis=1, keepdims=True) + EPS)
        queries[h * 256 : (h + 1) * 256, :] = (
            qh * r * score_gain[...] * (1.0 / math.sqrt(HD))
        ).astype(BF16)
    vx.wait_recv()
    vxr = vt.at[pl.ds(pl.multiple_of(jx * 32, 32), 32)]
    stale.append(copies(vxr, vxr, sibling))
    rows = pl.ds(pl.multiple_of(t * 16, 16), 16)
    for k in range(16):
        resid[:, k * 256 : (k + 1) * 256] = hid[k, rows, :].astype(F32)

    l_k.wait()
    l_v.wait()
    block = pl.ds(pl.multiple_of(s * 256, 256), 256)
    kv_at = y * 4 + zl
    old = jnp.concatenate([sk_own(kt, j, block), sk_own(vt, j, block)], axis=0)
    nkv[kv_at] = jnp.where(refresh[...] == 1, kv.astype(F32), old.astype(F32)).astype(BF16)
    kv_pair = copies(nkv.at[kv_at], nkv.at[kv_at], zpair)

    for copy in stale:
        copy.wait_recv()
    at("attention")
    total[...] = jnp.zeros_like(total)
    numer[...] = jnp.zeros_like(numer)

    def attend(kb, vb):
        kb = kb.astype(F32)
        r = lax.rsqrt(jnp.mean(kb * kb, axis=0, keepdims=True) + EPS)
        kn = (kb * r).astype(BF16)
        w = jnp.exp(jnp.dot(queries[...], kn, preferred_element_type=F32))
        total[...] += w[:, :128] + w[:, 128:]
        numer[...] += lax.dot_general(w.astype(BF16), vb, NT, preferred_element_type=F32)

    def other_block(i, carry):
        b = (s + 1 + i) % 16
        cols = pl.ds(pl.multiple_of(b * 256, 256), 256)
        attend(kt[:, cols], vt[:, cols])
        return carry

    lax.fori_loop(0, 15, other_block, 0)
    at("stale attended")
    for copy in for_mates:
        copy.wait_recv()
    fr = fresh[...]
    attend(fr[:, :32].reshape(128, 256), fr[:, 32:].reshape(128, 256))
    for h in range(2):
        hr = slice(h * 256, (h + 1) * 256)
        den = jnp.sum(total[hr, :], axis=1, keepdims=True)
        o = (numer[hr, :] / den).astype(BF16).reshape(8, 2, 16, HD)
        for cc in range(2):
            heads[cc * 128 : (cc + 1) * 128, h * HD : (h + 1) * HD] = o[:, cc].reshape(128, HD)

    def reduce_scatter(produce, sib_s, sib_r, own, xs, xr, zs, zr, zo, in_x, tag, finish):
        to_sib, to_x, to_z = [], [], []

        def along_x(k):
            to_sib[k].wait_recv()
            v = own[k] + sib_r[k].astype(F32).reshape(2, 4, 16, 1024)
            own[k] = v
            xs[k] = v.astype(BF16)
            to_x.append(
                [
                    copies(xs.at[k, :, (x + d) % 4], xr.at[k, d - 1], xdev(d))
                    for d in (1, 3, 2)
                ]
            )

        for k in range(NCH):
            v = produce(k)
            sib_s[k] = jnp.where(c == 0, v[128:], v[:128]).astype(BF16)
            to_sib.append(copies(sib_s.at[k], sib_r.at[k], sibling))
            own[k] = jnp.where(c == 0, v[:128], v[128:]).reshape(2, 4, 16, 1024)
            if k > 0:
                along_x(k - 1)
        along_x(NCH - 1)
        in_x()
        for k in range(NCH):
            v = own[k, :, x]
            for copy in to_x[k]:
                copy.wait_recv()
            for d in range(3):
                v = v + xr[k, d].astype(F32)
            zs[k] = jnp.where(zh == 0, v[1], v[0]).astype(BF16)
            zo[k] = jnp.where(zh == 0, v[0], v[1])
            to_z.append(copies(zs.at[k], zr.at[k], zpartner))
        at("sum along z" + tag)
        for k in range(NCH):
            to_z[k].wait_recv()
            finish(k, zo[k] + zr[k].astype(F32))

    l_o.wait()

    def project(k):
        return jnp.dot(
            heads[...], ow[:, k * 1024 : (k + 1) * 1024], preferred_element_type=F32
        )

    def add_attended(k, v):
        resid[:, k * 1024 : (k + 1) * 1024] += v

    at("attended")
    reduce_scatter(
        project, sib_s1, sib_r1, own1, xs1, xr1, zs1, zr1, zo1, lambda: at("sum along x"), "", add_attended
    )

    at("residual")
    kv_pair.wait_recv()
    duo = nkv.at[pl.ds(y * 4 + (zl // 2) * 2, 2)]
    kv_far = copies(duo, duo, zfar)
    v = resid[...]
    inv = lax.rsqrt(jnp.mean(v * v, axis=1, keepdims=True) + EPS)
    m = (v * inv * moe_gain[...]).astype(BF16)
    logits = lax.dot_general(router_t[...], m, NT, preferred_element_type=F32)
    expert = lax.broadcasted_iota(jnp.int32, (16, 16), 0)
    picked = jnp.zeros((16, 16), F32)
    for k in range(8):
        picked = picked + jnp.where(expert == ids_t[k : k + 1, :], 1.0, 0.0)
    sig = picked / (1.0 + jnp.exp(-logits))
    gates = 2.5 * sig / jnp.sum(sig, axis=0, keepdims=True)
    high = gates.astype(BF16).astype(F32)
    both = jnp.concatenate([high, gates - high, jnp.zeros((96, 16), F32)], axis=0)
    gates_rows = jnp.transpose(both).astype(BF16)
    for k in range(4):
        moe_in[k] = m[:, k * 1024 : (k + 1) * 1024]
    sigma = lambda zh_, x_, c_: c_ * 8 + zh_ * 4 + x_
    mine = sigma(zh, x, c)
    pay[:, :1024] = moe_in[1 - half]
    pay[:, 1024:2048] = moe_in[3 - half]
    swap = copies(pay, ag1.at[mine], zpair)
    ag0[mine, :, :1024] = moe_in[half]
    ag0[mine, :, 1024:2048] = moe_in[half + 2]
    ag0[mine, :, 2048:] = gates_rows
    g0 = gather_start(lambda *at_: ag0.at[sigma(*at_)], ag0.at[mine])
    swap.wait_recv()
    g1 = gather_start(lambda *at_: ag1.at[sigma(*at_)], ag1.at[mine])
    gather_z(g0)
    gather_x(g0, 0)
    gather_z(g1)
    at("far rows")
    gather_x(g1, 0)
    gather_x(g0, 1)
    gather_x(g1, 1)
    gather_end(g1)
    at("rows")

    l_gu.wait()
    for copy in ready["gu"]:
        copy.wait_recv()
    lane = lax.broadcasted_iota(jnp.int32, (256, 128), 1)
    is_mine = (lane == t) | (lane == t + 16)

    def partial(a, k, i):
        cols = slice(i * 1024 + k * 256, i * 1024 + (k + 1) * 256)
        return jnp.dot(a, gu[:, :, cols].reshape(2048, 256), preferred_element_type=F32)

    to_pair = []
    for k in range(4):
        for i in range(2):
            psend[k, i] = partial(ag1[...].reshape(256, 2048), k, i).astype(BF16)
        to_pair.append(copies(psend.at[k], precv.at[k], zpair))
    gather_end(g0)
    for k in range(4):
        for i in range(2):
            pown[k, i] = partial(ag0[:, :, :2048].reshape(256, 2048), k, i)
    w = ag0[:, :, 2048:].reshape(256, 128).astype(F32)
    gate = jnp.sum(jnp.where(is_mine, w, 0.0), axis=1, keepdims=True)
    at("partial sums")
    kv_far.wait_recv()
    quad = nkv.at[pl.ds(y * 4, 4)]
    kv_y = [copies(quad, quad, ydev(d)) for d in (1, 3, 2)]
    back = []
    for k in range(4):
        to_pair[k].wait_recv()
        g = pown[k, 0] + precv[k, 0].astype(F32)
        u = pown[k, 1] + precv[k, 1].astype(F32)
        act[0, k] = (g / (1.0 + jnp.exp(-g)) * u * gate).astype(BF16)
        back.append(copies(act.at[0, k], act.at[1, k], zfar))
        at("acted " + str(k))

    l_dn.wait()
    for copy in ready["dn"]:
        copy.wait_recv()

    def expert_out(k):
        b, run = k // 2, k % 2
        if k == 2:
            for copy in back:
                copy.wait_recv()
        outs = []
        for n in range(run * 4, run * 4 + 4):
            o = jnp.zeros((256, 256), F32)
            for i in range(4):
                o = o + jnp.dot(
                    act[b, i], dn[n, i * 256 : (i + 1) * 256, :], preferred_element_type=F32
                )
            outs.append(o)
        return jnp.concatenate(outs, axis=1)

    final = []

    def next_kv():
        for copy in kv_y:
            copy.wait_recv()
        for k in range(16):
            part = nkv[(k % 4) * 4 + k // 4]
            next_k[:, k * 256 : (k + 1) * 256] = part[:32]
            next_v[:, k * 256 : (k + 1) * 256] = part[32:]

    def place(k, v):
        if k < 2:
            cols = pl.ds(pl.multiple_of((2 * (zl // 2) + k) * 1024, 1024), 1024)
            mixed[:, cols] = (resid[:, cols] + v).astype(BF16)
        else:
            fsend[k - 2] = v.astype(BF16)
            final.append(copies(fsend.at[k - 2], frecv.at[k - 2], zfar))

    reduce_scatter(
        expert_out, sib_s2, sib_r2, own2, xs2, xr2, zs2, zr2, zo2, next_kv, " of experts", place
    )
    for k in range(2):
        final[k].wait_recv()
        cols = pl.ds(pl.multiple_of((2 - 2 * (zl // 2) + k) * 1024, 1024), 1024)
        mixed[:, cols] = (resid[:, cols] + frecv[k].astype(F32)).astype(BF16)

    for copy in copies.all:
        copy.wait_send()


def sk_own(ref, j, block):
    return ref[pl.ds(pl.multiple_of(j * 32, 32), 32), block]


def hand_over(a, b, c, a_out, b_out, c_out):
    a_out[...] = a[...]
    b_out[...] = b[...]
    c_out[...] = c[...]


def on_device(
    hidden,
    attn_gain,
    q_weight,
    k_weight,
    v_weight,
    out_weight,
    score_gain,
    stale_keys,
    stale_values,
    refresh,
    moe_gain,
    router,
    gate_up,
    down,
    expert_ids,
):
    anywhere = pl.BlockSpec(memory_space=pl.ANY)
    vmem = pl.BlockSpec(memory_space=pltpu.VMEM)

    rs = [
        pltpu.VMEM((NCH, 128, 1024), BF16),
        pltpu.VMEM((NCH, 128, 1024), BF16),
        pltpu.VMEM((NCH, 2, 4, 16, 1024), F32),
        pltpu.VMEM((NCH, 2, 4, 16, 1024), BF16),
        pltpu.VMEM((NCH, 3, 2, 16, 1024), BF16),
        pltpu.VMEM((NCH, 16, 1024), BF16),
        pltpu.VMEM((NCH, 16, 1024), BF16),
        pltpu.VMEM((NCH, 16, 1024), F32),
    ]

    mixed, next_k, next_v = pl.pallas_call(
        kernel,
        out_shape=(
            jax.ShapeDtypeStruct((16, 4096), BF16),
            jax.ShapeDtypeStruct((32, 4096), BF16),
            jax.ShapeDtypeStruct((32, 4096), BF16),
        ),
        in_specs=[
            anywhere,
            vmem,
            anywhere,
            vmem,
            vmem,
            anywhere,
            vmem,
            anywhere,
            anywhere,
            vmem,
            vmem,
            vmem,
            anywhere,
            anywhere,
            vmem,
        ],
        out_specs=(vmem, vmem, vmem),
        scratch_shapes=[
            pltpu.VMEM((16, 256, 256), BF16),
            pltpu.VMEM((4096, 256), BF16),
            pltpu.VMEM((256, 4096), BF16),
            pltpu.VMEM((128, 4096), BF16),
            pltpu.VMEM((128, 4096), BF16),
            pltpu.VMEM((512, 128), BF16),
            pltpu.VMEM((512, 128), F32),
            pltpu.VMEM((512, 128), F32),
            pltpu.VMEM((4, 64, 256), BF16),
            pltpu.VMEM((16, 64, 256), BF16),
            pltpu.VMEM((256, 256), BF16),
            pltpu.VMEM((16, 4096), F32),
            pltpu.VMEM((4, 16, 1024), BF16),
            pltpu.VMEM((16, 16, 2176), BF16),
            pltpu.VMEM((16, 16, 2048), BF16),
            pltpu.VMEM((16, 2048), BF16),
            pltpu.VMEM((8, 256, 2048), BF16),
            pltpu.VMEM((8, 1024, 256), BF16),
            pltpu.VMEM((4, 2, 256, 256), BF16),
            pltpu.VMEM((4, 2, 256, 256), BF16),
            pltpu.VMEM((4, 2, 256, 256), F32),
            pltpu.VMEM((2, 4, 256, 256), BF16),
            *rs,
            *rs,
            pltpu.VMEM((2, 16, 1024), BF16),
            pltpu.VMEM((2, 16, 1024), BF16),
            pltpu.SemaphoreType.DMA((COPIES,)),
            pltpu.SemaphoreType.DMA((COPIES,)),
            pltpu.SemaphoreType.DMA((8,)),
        ],
        compiler_params=pltpu.CompilerParams(
            collective_id=0, has_side_effects=True, vmem_limit_bytes=60 * 2**20
        ),
    )(
        hidden,
        attn_gain.reshape(1, -1),
        q_weight,
        k_weight.T,
        v_weight.T,
        out_weight,
        score_gain.reshape(1, -1),
        stale_keys.T,
        stale_values.T,
        refresh.reshape(1, -1),
        moe_gain.reshape(1, -1),
        router.T,
        gate_up[0],
        down[0],
        expert_ids.T,
    )
    results = (mixed, next_k, next_v)
    mixed, next_k, next_v = pl.pallas_call(
        hand_over,
        out_shape=tuple(jax.ShapeDtypeStruct(r.shape, r.dtype) for r in results),
        in_specs=[vmem] * 3,
        out_specs=(vmem,) * 3,
    )(*results)
    return (mixed, next_k.T, next_v.T)


def solution(mesh):
    placed = (
        P("seq", "tp"),
        P(),
        P(None, "tp"),
        P(None, "tp"),
        P(None, "tp"),
        P("tp", None),
        P(),
        P(None, "tp"),
        P(None, "tp"),
        P("seq"),
        P(),
        P(),
        P("tp", "seq", None),
        P("tp", None, "seq"),
        P(("seq", "tp"), None),
    )
    return jax.shard_map(
        on_device,
        mesh=mesh,
        in_specs=placed,
        out_specs=(P(("seq", "tp"), None), P(None, "tp"), P(None, "tp")),
        check_vma=False,
    )
```

```python
import functools
import math

import jax
import jax.numpy as jnp
from jax import lax
from jax.experimental import pallas as pl
from jax.experimental.pallas import tpu as pltpu
from jax.sharding import PartitionSpec as P

HD = 128
MESH = pl.DeviceIdType.MESH
F32 = jnp.float32
BF16 = jnp.bfloat16
NT = (((1,), (1,)), ((), ()))
EPS = 1e-06
NCH = 4
AHEAD = 2
COPIES = 160
SCHEDULE = {
    "start": [("gu", "near", 0, 256), ("gu", "z", 0, 128)],
    "far hidden": [("gu", "z", 128, 128)],
    "hidden": [("gu", "near on", 0, 256)],
    "attended": [("gu", "far", 0, 128)],
    "sum along z": [("gu", "far on", 0, 128), ("gu", "far", 128, 128)],
    "far rows": [("dn", "z", 0, 1024), ("gu", "far on", 128, 128)],
    "rows": [("dn", "near", 0, 1024)],
    "acted 0": [("dn", "far", 0, 1024)],
    "acted 1": [("dn", "near on", 0, 1024)],
    "acted 3": [("dn", "far on", 0, 1024)],
}


class Copies:
    def __init__(self, send, recv):
        self.send, self.recv, self.all = send, recv, []

    def __call__(self, src, dst, device):
        k = len(self.all)
        copy = pltpu.make_async_remote_copy(
            src_ref=src,
            dst_ref=dst,
            send_sem=self.send.at[k],
            recv_sem=self.recv.at[k],
            device_id=device,
            device_id_type=MESH,
        )
        copy.start()
        self.all.append(copy)
        return copy


def kernel(
    hidden,
    attn_gain,
    q_weight,
    kw_t,
    vw_t,
    out_weight,
    score_gain,
    sk_t,
    sv_t,
    refresh,
    moe_gain,
    router_t,
    gate_up,
    down,
    ids_t,
    mixed,
    next_k,
    next_v,
    hid,
    qw,
    ow,
    kt,
    vt,
    queries,
    total,
    numer,
    fresh,
    nkv,
    heads,
    resid,
    moe_in,
    ag0,
    ag1,
    pay,
    gu,
    dn,
    psend,
    precv,
    pown,
    act,
    sib_s1,
    sib_r1,
    own1,
    xs1,
    xr1,
    zs1,
    zr1,
    zo1,
    sib_s2,
    sib_r2,
    own2,
    xs2,
    xr2,
    zs2,
    zr2,
    zo2,
    fsend,
    frecv,
    send_sems,
    recv_sems,
    local_sems,
):
    s = lax.axis_index("seq")
    t = lax.axis_index("tp")
    y, zl = s % 4, s // 4
    zh, x, c = t // 8, (t // 2) % 4, t % 2
    half = zl % 2
    j = t % 4
    sibling = (s, t - c + (1 - c))
    zpartner = (s, (t + 8) % 16)
    xpair = x + 1 - 2 * (x % 2)
    xmate = (s, zh * 8 + xpair * 2 + c)
    xmate_sib = (s, zh * 8 + xpair * 2 + (1 - c))
    zpair = (s + 4 - 8 * half, t)
    zfar = ((s + 8) % 16, t)
    zpair_far = (s + 4 - 8 * half, (t + 8) % 16)
    zfar_far = ((s + 8) % 16, (t + 8) % 16)

    def xdev(d):
        return (s, zh * 8 + ((x + d) % 4) * 2 + c)

    def ydev(d):
        return (zl * 4 + (y + d) % 4, t)

    partners = [sibling, zpartner, xmate_sib, zpair, zfar, zpair_far, zfar_far]
    partners += [xdev(d) for d in (1, 2, 3)] + [ydev(d) for d in (1, 2, 3)]
    barrier = pltpu.get_barrier_semaphore()
    for device in partners:
        pl.semaphore_signal(barrier, inc=1, device_id=device, device_id_type=MESH)

    locals_ = []

    def local(src, dst):
        copy = pltpu.make_async_copy(src, dst, local_sems.at[len(locals_)])
        copy.start()
        locals_.append(copy)
        return copy

    l_hid = local(hidden, hid.at[t])
    l_k = local(sk_t, kt.at[pl.ds(pl.multiple_of(j * 32, 32), 32)])
    l_v = local(sv_t, vt.at[pl.ds(pl.multiple_of(j * 32, 32), 32)])
    l_q = local(q_weight, qw)
    l_o = local(out_weight, ow)
    own_gu = gu.at[(zl // 2) * 4 + y]
    own_dn = dn.at[half * 4 + y]
    l_gu = local(gate_up, own_gu)
    l_dn = local(down, own_dn)

    pl.semaphore_wait(barrier, len(partners))
    copies = Copies(send_sems, recv_sems)

    def gather_start(view, src):
        own = view(zh, x, c)
        over_z = copies(src, own, zpartner)
        over_x = {d: copies(src, own, xdev(d)) for d in (1, 3, 2)}
        return view, over_z, [(zh, over_x)], [copies(src, own, sibling)]

    def gather_from(view, near, over_z):
        near.wait_recv()
        own = view(zh, x, c)
        over_x = {d: copies(own, own, xdev(d)) for d in (1, 3, 2)}
        return view, over_z, [(zh, over_x)], [copies(own, own, sibling)]

    def gather_z(gather):
        view, over_z, over_x, to_sib = gather
        over_z.wait_recv()
        far = view(1 - zh, x, c)
        over_x.append((1 - zh, {d: copies(far, far, xdev(d)) for d in (1, 3, 2)}))
        to_sib.append(copies(far, far, sibling))

    def gather_x(gather, k):
        view, _, over_x, to_sib = gather
        z_of, group = over_x[k]
        for d in (1, 3, 2):
            group[d].wait_recv()
            part = view(z_of, (x + 4 - d) % 4, c)
            to_sib.append(copies(part, part, sibling))

    def gather_end(gather):
        for copy in gather[3]:
            copy.wait_recv()

    def ring_start(buf, src, zz, first, rows_):
        run = pl.ds(first, rows_)
        dst = buf.at[zz * 4 + y, run]
        return [copies(src.at[run], dst, ydev(d)) for d in (1, 3)]

    def ring_relay(buf, zz, first, rows_, started):
        sent = []
        for copy, d, start in zip(started, (1, 3), (first, first + rows_ // 2)):
            copy.wait_recv()
            part = buf.at[zz * 4 + (y + 4 - d) % 4, pl.ds(start, rows_ // 2)]
            sent.append(copies(part, part, ydev(d)))
        return sent

    bulk, ready = {}, {"gu": [], "dn": []}

    def at(point):
        for name, step, first, rows_ in SCHEDULE.get(point, ()):
            if name == "gu":
                buf, src, near, over = gu, gate_up, zl // 2, zfar
            else:
                buf, src, near, over = dn, down, half, zpair
            run = pl.ds(first, rows_)
            if step == "near":
                bulk[name, first] = ring_start(buf, src, near, first, rows_)
            elif step == "near on":
                ready[name] += ring_relay(buf, near, first, rows_, bulk[name, first])
            elif step == "z":
                own = buf.at[near * 4 + y, run]
                bulk[name, "z", first] = copies(src.at[run], own, over)
            elif step == "far":
                bulk[name, "z", first].wait_recv()
                far = buf.at[(1 - near) * 4 + y]
                bulk[name, "f", first] = ring_start(buf, far, 1 - near, first, rows_)
            else:
                ready[name] += ring_relay(
                    buf, 1 - near, first, rows_, bulk[name, "f", first]
                )

    gathers = []
    for first in (0, 128):
        rows_ = pl.ds(first, 128)
        gathers.append(
            gather_start(
                lambda zh_, x_, c_, rows_=rows_: hid.at[zh_ * 8 + x_ * 2 + c_, rows_],
                hidden.at[rows_],
            )
        )
    krows = kt.at[pl.ds(pl.multiple_of(j * 32, 32), 32)]
    vrows = vt.at[pl.ds(pl.multiple_of(j * 32, 32), 32)]
    kx = copies(sk_t, krows, xmate)
    stale = [copies(sk_t, krows, sibling), copies(sv_t, vrows, sibling)]
    at("start")
    for g in gathers:
        gather_z(g)
    vx = copies(sv_t, vrows, xmate)
    at("far hidden")
    for k in range(2):
        for g in gathers:
            gather_x(g, k)
    jx = (xpair % 2) * 2 + c
    kx.wait_recv()
    kxr = kt.at[pl.ds(pl.multiple_of(jx * 32, 32), 32)]
    stale.append(copies(kxr, kxr, sibling))
    for g in gathers:
        gather_end(g)
    l_hid.wait()
    at("hidden")

    l_q.wait()
    sq = jnp.zeros((256, 128), F32)
    for k in range(16):
        v = hid[k].astype(F32)
        v = v * v
        sq = sq + v[:, :128] + v[:, 128:]
    inv = lax.rsqrt(jnp.sum(sq, axis=1, keepdims=True) / 4096.0 + EPS)
    q = jnp.zeros((256, 256), F32)
    kv = jnp.zeros((64, 256), F32)
    for k in range(16):
        cols = slice(k * 256, (k + 1) * 256)
        n = (hid[k].astype(F32) * inv * attn_gain[:, cols]).astype(BF16)
        q = q + jnp.dot(n, qw[cols, :], preferred_element_type=F32)
        w = jnp.concatenate([kw_t[:, cols], vw_t[:, cols]], axis=0)
        kv = kv + lax.dot_general(w, n, NT, preferred_element_type=F32)
    kv = kv.astype(BF16)
    fresh[j] = kv
    for_mates = [copies(fresh.at[j], fresh.at[j], d) for d in (sibling, xmate, xmate_sib)]
    for h in range(2):
        qh = q[:, h * HD : (h + 1) * HD]
        r = lax.rsqrt(jnp.mean(qh * qh, axis=1, keepdims=True) + EPS)
        queries[h * 256 : (h + 1) * 256, :] = (
            qh * r * score_gain[...] * (1.0 / math.sqrt(HD))
        ).astype(BF16)
    vx.wait_recv()
    vxr = vt.at[pl.ds(pl.multiple_of(jx * 32, 32), 32)]
    stale.append(copies(vxr, vxr, sibling))
    rows = pl.ds(pl.multiple_of(t * 16, 16), 16)
    for k in range(16):
        resid[:, k * 256 : (k + 1) * 256] = hid[k, rows, :].astype(F32)

    l_k.wait()
    l_v.wait()
    block = pl.ds(pl.multiple_of(s * 256, 256), 256)
    kv_at = y * 4 + zl
    old = jnp.concatenate([sk_own(kt, j, block), sk_own(vt, j, block)], axis=0)
    nkv[kv_at] = jnp.where(refresh[...] == 1, kv.astype(F32), old.astype(F32)).astype(BF16)
    kv_pair = copies(nkv.at[kv_at], nkv.at[kv_at], zpair)

    for copy in stale:
        copy.wait_recv()
    at("attention")
    total[...] = jnp.zeros_like(total)
    numer[...] = jnp.zeros_like(numer)

    def attend(kb, vb):
        kb = kb.astype(F32)
        r = lax.rsqrt(jnp.mean(kb * kb, axis=0, keepdims=True) + EPS)
        kn = (kb * r).astype(BF16)
        w = jnp.exp(jnp.dot(queries[...], kn, preferred_element_type=F32))
        total[...] += w[:, :128] + w[:, 128:]
        numer[...] += lax.dot_general(w.astype(BF16), vb, NT, preferred_element_type=F32)

    def other_block(i, carry):
        b = (s + 1 + i) % 16
        cols = pl.ds(pl.multiple_of(b * 256, 256), 256)
        attend(kt[:, cols], vt[:, cols])
        return carry

    lax.fori_loop(0, 15, other_block, 0)
    at("stale attended")
    for copy in for_mates:
        copy.wait_recv()
    fr = fresh[...]
    attend(fr[:, :32].reshape(128, 256), fr[:, 32:].reshape(128, 256))
    for h in range(2):
        hr = slice(h * 256, (h + 1) * 256)
        den = jnp.sum(total[hr, :], axis=1, keepdims=True)
        o = (numer[hr, :] / den).astype(BF16).reshape(8, 2, 16, HD)
        for cc in range(2):
            heads[cc * 128 : (cc + 1) * 128, h * HD : (h + 1) * HD] = o[:, cc].reshape(128, HD)

    def reduce_scatter(produce, sib_s, sib_r, own, xs, xr, zs, zr, zo, in_x, tag, finish, near=NCH, beyond=None):
        to_sib, to_x, to_z = [], [], []

        def along_x(k):
            to_sib[k].wait_recv()
            v = own[k] + sib_r[k].astype(F32).reshape(2, 4, 16, 1024)
            own[k] = v
            xs[k] = v.astype(BF16)
            to_x.append(
                [
                    copies(xs.at[k, :, (x + d) % 4], xr.at[k, d - 1], xdev(d))
                    for d in (1, 3, 2)
                ]
            )

        for k in range(NCH):
            v = produce(k)
            sib_s[k] = jnp.where(c == 0, v[128:], v[:128]).astype(BF16)
            to_sib.append(copies(sib_s.at[k], sib_r.at[k], sibling))
            own[k] = jnp.where(c == 0, v[:128], v[128:]).reshape(2, 4, 16, 1024)
            if k > 0:
                along_x(k - 1)
        along_x(NCH - 1)
        in_x()
        for k in range(NCH):
            v = own[k, :, x]
            for copy in to_x[k]:
                copy.wait_recv()
            for d in range(3):
                v = v + xr[k, d].astype(F32)
            zs[k] = jnp.where(zh == 0, v[1], v[0]).astype(BF16)
            zo[k] = jnp.where(zh == 0, v[0], v[1])
            if k < near:
                to_z.append(copies(zs.at[k], zr.at[k], zpartner))
            else:
                beyond(k - near, zs.at[k], zo[k])
        at("sum along z" + tag)
        for k in range(near):
            to_z[k].wait_recv()
            finish(k, zo[k] + zr[k].astype(F32))

    l_o.wait()

    def project(k):
        return jnp.dot(
            heads[...], ow[:, k * 1024 : (k + 1) * 1024], preferred_element_type=F32
        )

    def add_attended(k, v):
        resid[:, k * 1024 : (k + 1) * 1024] += v

    at("attended")
    reduce_scatter(
        project, sib_s1, sib_r1, own1, xs1, xr1, zs1, zr1, zo1, lambda: at("sum along x"), "", add_attended
    )

    at("residual")
    kv_pair.wait_recv()
    duo = nkv.at[pl.ds(y * 4 + (zl // 2) * 2, 2)]
    kv_far = copies(duo, duo, zfar)
    v = resid[...]
    inv = lax.rsqrt(jnp.mean(v * v, axis=1, keepdims=True) + EPS)
    m = (v * inv * moe_gain[...]).astype(BF16)
    logits = lax.dot_general(router_t[...], m, NT, preferred_element_type=F32)
    expert = lax.broadcasted_iota(jnp.int32, (16, 16), 0)
    picked = jnp.zeros((16, 16), F32)
    for k in range(8):
        picked = picked + jnp.where(expert == ids_t[k : k + 1, :], 1.0, 0.0)
    sig = picked / (1.0 + jnp.exp(-logits))
    gates = 2.5 * sig / jnp.sum(sig, axis=0, keepdims=True)
    high = gates.astype(BF16).astype(F32)
    both = jnp.concatenate([high, gates - high, jnp.zeros((96, 16), F32)], axis=0)
    gates_rows = jnp.transpose(both).astype(BF16)
    for k in range(4):
        moe_in[k] = m[:, k * 1024 : (k + 1) * 1024]
    sigma = lambda zh_, x_, c_: c_ * 8 + zh_ * 4 + x_
    mine = sigma(zh, x, c)
    pay[:, :1024] = moe_in[1 - half]
    pay[:, 1024:2048] = moe_in[3 - half]
    swap = copies(pay, ag1.at[mine], zpair)
    swap_far = copies(pay, ag1.at[mine], zpair_far)
    ag0[mine, :, :1024] = moe_in[half]
    ag0[mine, :, 1024:2048] = moe_in[half + 2]
    ag0[mine, :, 2048:] = gates_rows
    g0 = gather_start(lambda *at_: ag0.at[sigma(*at_)], ag0.at[mine])
    g1 = gather_from(lambda *at_: ag1.at[sigma(*at_)], swap, swap_far)
    gather_z(g1)
    gather_z(g0)
    at("far rows")
    gather_x(g0, 0)
    gather_x(g1, 0)
    gather_x(g1, 1)
    gather_x(g0, 1)
    gather_end(g1)
    at("rows")

    l_gu.wait()
    for copy in ready["gu"]:
        copy.wait_recv()
    lane = lax.broadcasted_iota(jnp.int32, (256, 128), 1)
    is_mine = (lane == t) | (lane == t + 16)

    def partial(a, k, i):
        cols = slice(i * 1024 + k * 256, i * 1024 + (k + 1) * 256)
        return jnp.dot(a, gu[:, :, cols].reshape(2048, 256), preferred_element_type=F32)

    to_pair = []
    for k in range(4):
        for i in range(2):
            psend[k, i] = partial(ag1[...].reshape(256, 2048), k, i).astype(BF16)
        if k < AHEAD:
            to_pair.append(copies(psend.at[k], precv.at[k], zpair))
    gather_end(g0)
    for k in range(4):
        for i in range(2):
            pown[k, i] = partial(ag0[:, :, :2048].reshape(256, 2048), k, i)
    w = ag0[:, :, 2048:].reshape(256, 128).astype(F32)
    gate = jnp.sum(jnp.where(is_mine, w, 0.0), axis=1, keepdims=True)
    at("partial sums")
    kv_far.wait_recv()
    quad = nkv.at[pl.ds(y * 4, 4)]
    kv_y = [copies(quad, quad, ydev(d)) for d in (1, 3, 2)]
    back = []
    for k in range(4):
        to_pair[k].wait_recv()
        g = pown[k, 0] + precv[k, 0].astype(F32)
        u = pown[k, 1] + precv[k, 1].astype(F32)
        act[0, k] = (g / (1.0 + jnp.exp(-g)) * u * gate).astype(BF16)
        back.append(copies(act.at[0, k], act.at[1, k], zfar))
        if k + AHEAD < 4:
            to_pair.append(copies(psend.at[k + AHEAD], precv.at[k + AHEAD], zpair))
        at("acted " + str(k))

    l_dn.wait()
    for copy in ready["dn"]:
        copy.wait_recv()

    def expert_out(k):
        b, run = k // 2, k % 2
        if k == 2:
            for copy in back:
                copy.wait_recv()
        outs = []
        for n in range(run * 4, run * 4 + 4):
            o = jnp.zeros((256, 256), F32)
            for i in range(4):
                o = o + jnp.dot(
                    act[b, i], dn[n, i * 256 : (i + 1) * 256, :], preferred_element_type=F32
                )
            outs.append(o)
        return jnp.concatenate(outs, axis=1)

    final = []

    def next_kv():
        for copy in kv_y:
            copy.wait_recv()
        for k in range(16):
            part = nkv[(k % 4) * 4 + k // 4]
            next_k[:, k * 256 : (k + 1) * 256] = part[:32]
            next_v[:, k * 256 : (k + 1) * 256] = part[32:]

    def place(k, v):
        cols = pl.ds(pl.multiple_of((2 * (zl // 2) + k) * 1024, 1024), 1024)
        mixed[:, cols] = (resid[:, cols] + v).astype(BF16)

    def to_owners(k, other, own):
        fsend[k] = own.astype(BF16)
        a = copies(fsend.at[k], frecv.at[k, 0], zfar)
        b = copies(other, frecv.at[k, 1], zfar_far)
        final.append((a, b))

    reduce_scatter(
        expert_out, sib_s2, sib_r2, own2, xs2, xr2, zs2, zr2, zo2, next_kv, " of experts", place, 2, to_owners
    )
    for k in range(2):
        for copy in final[k]:
            copy.wait_recv()
        v = frecv[k, 0].astype(F32) + frecv[k, 1].astype(F32)
        cols = pl.ds(pl.multiple_of((2 - 2 * (zl // 2) + k) * 1024, 1024), 1024)
        mixed[:, cols] = (resid[:, cols] + v).astype(BF16)

    for copy in copies.all:
        copy.wait_send()


def sk_own(ref, j, block):
    return ref[pl.ds(pl.multiple_of(j * 32, 32), 32), block]


def hand_over(a, b, c, a_out, b_out, c_out):
    a_out[...] = a[...]
    b_out[...] = b[...]
    c_out[...] = c[...]


def on_device(
    hidden,
    attn_gain,
    q_weight,
    k_weight,
    v_weight,
    out_weight,
    score_gain,
    stale_keys,
    stale_values,
    refresh,
    moe_gain,
    router,
    gate_up,
    down,
    expert_ids,
):
    anywhere = pl.BlockSpec(memory_space=pl.ANY)
    vmem = pl.BlockSpec(memory_space=pltpu.VMEM)

    rs = [
        pltpu.VMEM((NCH, 128, 1024), BF16),
        pltpu.VMEM((NCH, 128, 1024), BF16),
        pltpu.VMEM((NCH, 2, 4, 16, 1024), F32),
        pltpu.VMEM((NCH, 2, 4, 16, 1024), BF16),
        pltpu.VMEM((NCH, 3, 2, 16, 1024), BF16),
        pltpu.VMEM((NCH, 16, 1024), BF16),
        pltpu.VMEM((NCH, 16, 1024), BF16),
        pltpu.VMEM((NCH, 16, 1024), F32),
    ]

    mixed, next_k, next_v = pl.pallas_call(
        kernel,
        out_shape=(
            jax.ShapeDtypeStruct((16, 4096), BF16),
            jax.ShapeDtypeStruct((32, 4096), BF16),
            jax.ShapeDtypeStruct((32, 4096), BF16),
        ),
        in_specs=[
            anywhere,
            vmem,
            anywhere,
            vmem,
            vmem,
            anywhere,
            vmem,
            anywhere,
            anywhere,
            vmem,
            vmem,
            vmem,
            anywhere,
            anywhere,
            vmem,
        ],
        out_specs=(vmem, vmem, vmem),
        scratch_shapes=[
            pltpu.VMEM((16, 256, 256), BF16),
            pltpu.VMEM((4096, 256), BF16),
            pltpu.VMEM((256, 4096), BF16),
            pltpu.VMEM((128, 4096), BF16),
            pltpu.VMEM((128, 4096), BF16),
            pltpu.VMEM((512, 128), BF16),
            pltpu.VMEM((512, 128), F32),
            pltpu.VMEM((512, 128), F32),
            pltpu.VMEM((4, 64, 256), BF16),
            pltpu.VMEM((16, 64, 256), BF16),
            pltpu.VMEM((256, 256), BF16),
            pltpu.VMEM((16, 4096), F32),
            pltpu.VMEM((4, 16, 1024), BF16),
            pltpu.VMEM((16, 16, 2176), BF16),
            pltpu.VMEM((16, 16, 2048), BF16),
            pltpu.VMEM((16, 2048), BF16),
            pltpu.VMEM((8, 256, 2048), BF16),
            pltpu.VMEM((8, 1024, 256), BF16),
            pltpu.VMEM((4, 2, 256, 256), BF16),
            pltpu.VMEM((4, 2, 256, 256), BF16),
            pltpu.VMEM((4, 2, 256, 256), F32),
            pltpu.VMEM((2, 4, 256, 256), BF16),
            *rs,
            *rs,
            pltpu.VMEM((2, 16, 1024), BF16),
            pltpu.VMEM((2, 2, 16, 1024), BF16),
            pltpu.SemaphoreType.DMA((COPIES,)),
            pltpu.SemaphoreType.DMA((COPIES,)),
            pltpu.SemaphoreType.DMA((8,)),
        ],
        compiler_params=pltpu.CompilerParams(
            collective_id=0, has_side_effects=True, vmem_limit_bytes=60 * 2**20
        ),
    )(
        hidden,
        attn_gain.reshape(1, -1),
        q_weight,
        k_weight.T,
        v_weight.T,
        out_weight,
        score_gain.reshape(1, -1),
        stale_keys.T,
        stale_values.T,
        refresh.reshape(1, -1),
        moe_gain.reshape(1, -1),
        router.T,
        gate_up[0],
        down[0],
        expert_ids.T,
    )
    results = (mixed, next_k, next_v)
    mixed, next_k, next_v = pl.pallas_call(
        hand_over,
        out_shape=tuple(jax.ShapeDtypeStruct(r.shape, r.dtype) for r in results),
        in_specs=[vmem] * 3,
        out_specs=(vmem,) * 3,
    )(*results)
    return (mixed, next_k.T, next_v.T)


def solution(mesh):
    placed = (
        P("seq", "tp"),
        P(),
        P(None, "tp"),
        P(None, "tp"),
        P(None, "tp"),
        P("tp", None),
        P(),
        P(None, "tp"),
        P(None, "tp"),
        P("seq"),
        P(),
        P(),
        P("tp", "seq", None),
        P("tp", None, "seq"),
        P(("seq", "tp"), None),
    )
    return jax.shard_map(
        on_device,
        mesh=mesh,
        in_specs=placed,
        out_specs=(P(("seq", "tp"), None), P(None, "tp"), P(None, "tp")),
        check_vma=False,
    )
```
